32 devices in a mesh: seq: 32 (over z, y, x, core), batch: 1.
Axes of the slice: x: 2, y: 2, z: 4, core: 2. Of those that a mesh axis runs over, the one named last changes fastest.
Arguments:
- tokens: bfloat16 [1, 131072, 1024], P('batch', 'seq'), may hold values from -6 to 6
- cotangent: bfloat16 [1, 131072, 1024], P('batch', 'seq'), may hold values from -6 to 6
- left_factor: bfloat16 [512, 256, 256], P('seq'), may hold values from -0.375 to 0.375
- right_factor: bfloat16 [256, 512, 512], P('seq'), may hold values from -0.25 to 0.25
Outputs:
- output: bfloat16 [1, 131072, 1024], P('batch', 'seq')
- tokens_grad: bfloat16 [1, 131072, 1024], P('batch', 'seq')
- left_grad: float32 [512, 256, 256], P('seq', 'batch')
- right_grad: float32 [256, 512, 512], P('seq', 'batch')
The draws below stay inside these ranges and needn't reach their ends.
All inputs are finite; a program needn't handle non-finite values.
Results may differ from the reference program's by a relative error of at most 0.0058.
Values may be sent and summed in bfloat16 or wider, within the bound.
A program may use at most 192 MiB of HBM per device.

```python
import jax
import jax.numpy as jnp
from jax import lax

M1 = 512
M2 = 256
D = 1024
SEQLEN = 131072
BATCH = 1


def block_scale(own_key, shape, shards, low, top_value):
    def one(axis_at, blocks):
        draws = jax.random.uniform(jax.random.fold_in(jax.random.fold_in(own_key, 6), axis_at), (blocks,), jnp.float32, low / len(shards), top_value / len(shards))
        return jnp.repeat(jnp.exp(draws), shape[axis_at] // blocks).reshape((-1,) + (1,) * (len(shape) - axis_at - 1))

    loudness = one(*shards[0])
    for cut in shards[1:]:
        loudness = loudness * one(*cut)
    return loudness


def bell_draw(own_key, extent, width, reach, split=(), dtype=jnp.bfloat16):
    values = jax.random.normal(own_key, extent, jnp.float32) * width
    if len(split) > 0:
        values = block_scale(own_key, extent, split, -0.22, 0.18) * values
    return jnp.clip(values, min=-reach, max=reach).astype(dtype)


def setup_inputs(seed: int = 0) -> dict:
    key_of = jax.random.split(jax.random.key(seed), 5)
    tokens = bell_draw(key_of[0], (BATCH, SEQLEN, D), 1.0, 6.0, ((1, 32),))
    cotangent = bell_draw(key_of[1], (BATCH, SEQLEN, D), 1.0, 6.0, ((1, 32),))
    left_factor = bell_draw(key_of[2], (M1, M2, M2), M2 ** -0.5, 0.375, ((0, 32),))
    right_factor = bell_draw(key_of[3], (M2, M1, M1), M1 ** -0.5, 0.25, ((0, 32),))
    return {"tokens": tokens, "cotangent": cotangent, "left_factor": left_factor, "right_factor": right_factor}


grad_unscale = 1.0 / 32.0


def reference(tokens, cotangent, left_factor, right_factor):
    global_left = left_factor.astype(jnp.float32)
    global_right = right_factor.astype(jnp.float32)

    def step(carry, pair):
        left_sum, right_sum = carry
        seq_x, seq_g = pair
        blocks = seq_x.reshape(M1, M2, D)
        upstream = seq_g.reshape(M1, M2, D).astype(jnp.float32)
        tokens_f = blocks.astype(jnp.float32)
        first = jnp.einsum('apq,aqd->apd', global_left, tokens_f).astype(jnp.bfloat16)
        second = jnp.einsum('bij,jbd->ibd', global_right, first.astype(jnp.float32)).astype(jnp.bfloat16)
        gate_sig = jax.nn.sigmoid(tokens_f)
        silu_x = tokens_f * gate_sig
        second_f = second.astype(jnp.float32)
        output = (second_f * silu_x).astype(jnp.bfloat16)
        grad_second = (upstream * silu_x).astype(jnp.bfloat16)
        grad_first = jnp.einsum('bij,ibd->jbd', global_right, grad_second.astype(jnp.float32)).astype(jnp.bfloat16)
        right_term = jnp.einsum('ibd,jbd->bij', grad_second.astype(jnp.float32), first.astype(jnp.float32))
        left_term = jnp.einsum('apd,aqd->apq', grad_first.astype(jnp.float32), tokens_f)
        gate_grad = upstream * second_f * gate_sig * (1.0 + tokens_f * (1.0 - gate_sig))
        tokens_grad = (jnp.einsum('apq,apd->aqd', global_left, grad_first.astype(jnp.float32)) + gate_grad).astype(jnp.bfloat16)
        return (left_sum + left_term, right_sum + right_term), (output.reshape(M1 * M2, D), tokens_grad.reshape(M1 * M2, D))

    start = (jnp.zeros((M1, M2, M2), jnp.float32), jnp.zeros((M2, M1, M1), jnp.float32))
    sums, stacked = lax.scan(step, start, (tokens, cotangent))
    left_grad = sums[0] * grad_unscale
    right_grad = sums[1] * grad_unscale
    return stacked[0], stacked[1], left_grad, right_grad
```

```python
import functools

import jax
import jax.numpy as jnp
from jax import lax
from jax.experimental import pallas as pl
from jax.experimental.pallas import tpu as pltpu
from jax.sharding import PartitionSpec as P

grad_unscale = 1.0 / 32.0


def plain_shards(tokens, cotangent, left_factor, right_factor):
    a_rows = left_factor.shape[0]
    block_len = left_factor.shape[1]
    channels = tokens.shape[2]
    blocks = tokens.reshape(a_rows, block_len, channels)
    upstream = cotangent.reshape(a_rows, block_len, channels).astype(jnp.float32)
    tokens_f = blocks.astype(jnp.float32)
    gate_sig = jax.nn.sigmoid(tokens_f)
    silu_x = tokens_f * gate_sig
    first = jnp.einsum(
        "apq,aqd->apd", left_factor, blocks, preferred_element_type=jnp.float32
    ).astype(jnp.bfloat16)
    grad_second = (upstream * silu_x).astype(jnp.bfloat16)
    first_cols = lax.all_to_all(first, "seq", split_axis=1, concat_axis=0, tiled=True)
    first_cols, second = (
        first_cols,
        lax.all_to_all(
            jnp.einsum(
                "bij,jbd->ibd", right_factor, first_cols, preferred_element_type=jnp.float32
            ).astype(jnp.bfloat16),
            "seq",
            split_axis=0,
            concat_axis=1,
            tiled=True,
        ),
    )
    grad_cols = lax.all_to_all(grad_second, "seq", split_axis=1, concat_axis=0, tiled=True)
    grad_cols, grad_first = (
        grad_cols,
        lax.all_to_all(
            jnp.einsum(
                "bij,ibd->jbd", right_factor, grad_cols, preferred_element_type=jnp.float32
            ).astype(jnp.bfloat16),
            "seq",
            split_axis=0,
            concat_axis=1,
            tiled=True,
        ),
    )
    right_term = jnp.einsum(
        "ibd,jbd->bij", grad_cols, first_cols, preferred_element_type=jnp.float32
    )
    right_grad = (
        lax.psum_scatter(right_term, "batch", scatter_dimension=1, tiled=True) * grad_unscale
    )
    second_f = second.astype(jnp.float32)
    output = (second_f * silu_x).astype(jnp.bfloat16)
    gate_grad = upstream * second_f * gate_sig * (1.0 + tokens_f * (1.0 - gate_sig))
    tokens_grad = (
        jnp.einsum("apq,apd->aqd", left_factor, grad_first, preferred_element_type=jnp.float32)
        + gate_grad
    ).astype(jnp.bfloat16)
    left_term = jnp.einsum("apd,aqd->apq", grad_first, blocks, preferred_element_type=jnp.float32)
    left_grad = lax.psum_scatter(left_term, "batch", scatter_dimension=1, tiled=True) * grad_unscale
    return (output.reshape(tokens.shape), tokens_grad.reshape(tokens.shape), left_grad, right_grad)


def exchange(parts):
    return lax.all_to_all(parts, "seq", split_axis=0, concat_axis=0, tiled=True)


def after(value, *others):
    return lax.optimization_barrier((value,) + others)[0]


def call(kernel, n, in_specs, out_specs, out_shape, cost, aliases=None):
    return pl.pallas_call(
        kernel,
        grid=(n,),
        in_specs=in_specs,
        out_specs=out_specs,
        out_shape=out_shape,
        input_output_aliases=aliases or {},
        cost_estimate=pl.CostEstimate(flops=cost[0], bytes_accessed=cost[1], transcendentals=0),
        compiler_params=pltpu.CompilerParams(vmem_limit_bytes=48 * 1024 * 1024),
    )


def row_spec(rows, columns, lo=0):
    return pl.BlockSpec((1, rows, columns), lambda a: (a + lo, 0, 0))


def split_spec(devices, b_rows, channels, lo=0):
    return pl.BlockSpec((devices, 1, b_rows, channels), lambda a: (0, a + lo, 0, 0))


def store_split(out_ref, value):
    devices, _, b_rows, channels = out_ref.shape
    out_ref[:, 0] = value.reshape(devices, b_rows, channels).astype(out_ref.dtype)


def load_split(in_ref):
    devices, _, b_rows, channels = in_ref.shape
    return in_ref[:, 0].astype(jnp.float32).reshape(devices * b_rows, channels)


def first_kernel(l_ref, x_ref, o_ref):
    store_split(o_ref, jnp.dot(l_ref[0], x_ref[0], preferred_element_type=jnp.float32))


def grad_second_kernel(x_ref, g_ref, o_ref):
    x = x_ref[0].astype(jnp.float32)
    store_split(o_ref, g_ref[0].astype(jnp.float32) * (x * jax.nn.sigmoid(x)))


def output_kernel(x_ref, second_ref, o_ref):
    x = x_ref[0].astype(jnp.float32)
    o_ref[0] = (load_split(second_ref) * (x * jax.nn.sigmoid(x))).astype(o_ref.dtype)


def last_kernel(l_ref, x_ref, g_ref, second_ref, grad_ref, *rest):
    tokens_grad_ref, left_ref = rest[-2:]
    x = x_ref[0].astype(jnp.float32)
    s = jax.nn.sigmoid(x)
    gate = g_ref[0].astype(jnp.float32) * load_split(second_ref) * s * (1.0 + x * (1.0 - s))
    grad_first = load_split(grad_ref).astype(jnp.bfloat16)
    back = lax.dot_general(
        l_ref[0], grad_first, (((0,), (0,)), ((), ())), preferred_element_type=jnp.float32
    )
    tokens_grad_ref[0] = (back + gate).astype(tokens_grad_ref.dtype)
    left_term = lax.dot_general(
        grad_first, x_ref[0], (((1,), (1,)), ((), ())), preferred_element_type=jnp.float32
    )
    left_ref[0] = left_term * grad_unscale


def shards(tokens, cotangent, left_factor, right_factor):
    a_rows, block_len, _ = left_factor.shape
    b_rows = right_factor.shape[0]
    channels = tokens.shape[2]
    devices = block_len // b_rows
    if b_rows % 8 or a_rows % 4 or tokens.shape[0] != 1:
        return plain_shards(tokens, cotangent, left_factor, right_factor)
    head = a_rows // 4
    tail = a_rows - head
    x = tokens.reshape(a_rows, block_len, channels)
    g = cotangent.reshape(a_rows, block_len, channels)
    row_bytes = block_len * channels * 2
    row_flops = 2 * block_len * block_len * channels
    row = functools.partial(row_spec, block_len, channels)
    square = functools.partial(row_spec, block_len, block_len)
    split = functools.partial(split_spec, devices, b_rows, channels)

    def split_shape(n):
        return jax.ShapeDtypeStruct((devices, n, b_rows, channels), jnp.bfloat16)

    def first_part(lo, n):
        return call(
            first_kernel,
            n,
            [square(lo), row(lo)],
            split(),
            split_shape(n),
            (n * row_flops, 2 * n * row_bytes),
        )(left_factor, x)

    first_0 = exchange(first_part(0, head))
    first_1 = exchange(after(first_part(head, tail), first_0))
    grad_second = call(
        grad_second_kernel,
        a_rows,
        [row(), row()],
        split(),
        split_shape(a_rows),
        (a_rows * row_bytes * 5, 3 * a_rows * row_bytes),
    )(x, g)
    grad_cols = exchange(after(grad_second, first_0)).reshape(devices * a_rows, b_rows, channels)
    first_cols = jnp.concatenate([first_0, first_1], axis=1).reshape(
        devices * a_rows, b_rows, channels
    )
    second_cols = jnp.einsum(
        "bij,jbd->ibd", right_factor, first_cols, preferred_element_type=jnp.float32
    ).astype(jnp.bfloat16)
    second = exchange(second_cols.reshape(devices, a_rows, b_rows, channels))
    grad_rows = (
        jnp.einsum("bij,ibd->jbd", right_factor, grad_cols, preferred_element_type=jnp.float32)
        .astype(jnp.bfloat16)
        .reshape(devices, a_rows, b_rows, channels)
    )
    grad_first_0 = exchange(grad_rows[:, :tail])
    right_term = jnp.einsum(
        "ibd,jbd->bij", grad_cols, first_cols, preferred_element_type=jnp.float32
    )
    right_grad = (
        lax.psum_scatter(right_term, "batch", scatter_dimension=1, tiled=True) * grad_unscale
    )
    output = call(
        output_kernel,
        a_rows,
        [row(), split()],
        row(),
        jax.ShapeDtypeStruct(x.shape, jnp.bfloat16),
        (a_rows * row_bytes * 5, 3 * a_rows * row_bytes),
    )(x, second)
    grad_first_0, output, right_grad = lax.optimization_barrier(
        (grad_first_0, output, right_grad)
    )
    grad_first_1 = exchange(after(grad_rows[:, tail:], grad_first_0))

    def last_part(lo, n, grad_first, *held):
        return call(
            last_kernel,
            n,
            [square(lo), row(lo), row(lo), split(lo), split()]
            + [pl.BlockSpec(memory_space=pl.ANY)] * len(held),
            (row(lo), square(lo)),
            (
                jax.ShapeDtypeStruct(x.shape, jnp.bfloat16),
                jax.ShapeDtypeStruct(left_factor.shape, jnp.float32),
            ),
            (2 * n * row_flops, 5 * n * row_bytes),
            {5 + k: k for k in range(len(held))},
        )(left_factor, x, g, second, grad_first, *held)

    held = last_part(0, tail, grad_first_0)
    grad_first_1, *held = lax.optimization_barrier((grad_first_1, *held))
    tokens_grad, left_term = last_part(tail, head, grad_first_1, *held)
    left_grad = lax.psum_scatter(left_term, "batch", scatter_dimension=1, tiled=True)
    return (output.reshape(tokens.shape), tokens_grad.reshape(tokens.shape), left_grad, right_grad)


def solution(mesh):
    return jax.shard_map(
        shards,
        mesh=mesh,
        in_specs=(
            P("batch", "seq", None),
            P("batch", "seq", None),
            P("seq", None, None),
            P("seq", None, None),
        ),
        out_specs=(
            P("batch", "seq", None),
            P("batch", "seq", None),
            P("seq", "batch", None),
            P("seq", "batch", None),
        ),
        check_vma=False,
    )
```

```python
import functools

import jax
import jax.numpy as jnp
from jax import lax
from jax.experimental import pallas as pl
from jax.experimental.pallas import tpu as pltpu
from jax.sharding import PartitionSpec as P

grad_unscale = 1.0 / 32.0


def plain_shards(tokens, cotangent, left_factor, right_factor):
    a_rows = left_factor.shape[0]
    block_len = left_factor.shape[1]
    channels = tokens.shape[2]
    blocks = tokens.reshape(a_rows, block_len, channels)
    upstream = cotangent.reshape(a_rows, block_len, channels).astype(jnp.float32)
    tokens_f = blocks.astype(jnp.float32)
    gate_sig = jax.nn.sigmoid(tokens_f)
    silu_x = tokens_f * gate_sig
    first = jnp.einsum(
        "apq,aqd->apd", left_factor, blocks, preferred_element_type=jnp.float32
    ).astype(jnp.bfloat16)
    grad_second = (upstream * silu_x).astype(jnp.bfloat16)
    first_cols = lax.all_to_all(first, "seq", split_axis=1, concat_axis=0, tiled=True)
    first_cols, second = (
        first_cols,
        lax.all_to_all(
            jnp.einsum(
                "bij,jbd->ibd", right_factor, first_cols, preferred_element_type=jnp.float32
            ).astype(jnp.bfloat16),
            "seq",
            split_axis=0,
            concat_axis=1,
            tiled=True,
        ),
    )
    grad_cols = lax.all_to_all(grad_second, "seq", split_axis=1, concat_axis=0, tiled=True)
    grad_cols, grad_first = (
        grad_cols,
        lax.all_to_all(
            jnp.einsum(
                "bij,ibd->jbd", right_factor, grad_cols, preferred_element_type=jnp.float32
            ).astype(jnp.bfloat16),
            "seq",
            split_axis=0,
            concat_axis=1,
            tiled=True,
        ),
    )
    right_term = jnp.einsum(
        "ibd,jbd->bij", grad_cols, first_cols, preferred_element_type=jnp.float32
    )
    right_grad = (
        lax.psum_scatter(right_term, "batch", scatter_dimension=1, tiled=True) * grad_unscale
    )
    second_f = second.astype(jnp.float32)
    output = (second_f * silu_x).astype(jnp.bfloat16)
    gate_grad = upstream * second_f * gate_sig * (1.0 + tokens_f * (1.0 - gate_sig))
    tokens_grad = (
        jnp.einsum("apq,apd->aqd", left_factor, grad_first, preferred_element_type=jnp.float32)
        + gate_grad
    ).astype(jnp.bfloat16)
    left_term = jnp.einsum("apd,aqd->apq", grad_first, blocks, preferred_element_type=jnp.float32)
    left_grad = lax.psum_scatter(left_term, "batch", scatter_dimension=1, tiled=True) * grad_unscale
    return (output.reshape(tokens.shape), tokens_grad.reshape(tokens.shape), left_grad, right_grad)


def exchange(parts):
    return lax.all_to_all(parts, "seq", split_axis=0, concat_axis=0, tiled=True)


def after(value, *others):
    return lax.optimization_barrier((value,) + others)[0]


def call(kernel, n, in_specs, out_specs, out_shape, cost, aliases=None, vmem_mib=48):
    return pl.pallas_call(
        kernel,
        grid=(n,),
        in_specs=in_specs,
        out_specs=out_specs,
        out_shape=out_shape,
        input_output_aliases=aliases or {},
        cost_estimate=pl.CostEstimate(flops=cost[0], bytes_accessed=cost[1], transcendentals=0),
        compiler_params=pltpu.CompilerParams(vmem_limit_bytes=vmem_mib * 1024 * 1024),
    )


def row_spec(rows, columns, lo=0):
    return pl.BlockSpec((1, rows, columns), lambda a: (a + lo, 0, 0))


def split_spec(devices, b_rows, channels, lo=0):
    return pl.BlockSpec((devices, 1, b_rows, channels), lambda a: (0, a + lo, 0, 0))


def store_split(out_ref, value):
    devices, _, b_rows, channels = out_ref.shape
    out_ref[:, 0] = value.reshape(devices, b_rows, channels).astype(out_ref.dtype)


def load_split(in_ref):
    devices, _, b_rows, channels = in_ref.shape
    return in_ref[:, 0].astype(jnp.float32).reshape(devices * b_rows, channels)


def first_kernel(l_ref, x_ref, o_ref):
    store_split(o_ref, jnp.dot(l_ref[0], x_ref[0], preferred_element_type=jnp.float32))


def grad_second_kernel(x_ref, g_ref, o_ref):
    x = x_ref[0].astype(jnp.float32)
    store_split(o_ref, g_ref[0].astype(jnp.float32) * (x * jax.nn.sigmoid(x)))


def output_kernel(x_ref, second_ref, o_ref):
    x = x_ref[0].astype(jnp.float32)
    o_ref[0] = (load_split(second_ref) * (x * jax.nn.sigmoid(x))).astype(o_ref.dtype)


def last_kernel(l_ref, x_ref, g_ref, second_ref, grad_ref, *rest):
    tokens_grad_ref, left_ref = rest[-2:]
    x = x_ref[0].astype(jnp.float32)
    s = jax.nn.sigmoid(x)
    gate = g_ref[0].astype(jnp.float32) * load_split(second_ref) * s * (1.0 + x * (1.0 - s))
    grad_first = load_split(grad_ref).astype(jnp.bfloat16)
    back = lax.dot_general(
        l_ref[0], grad_first, (((0,), (0,)), ((), ())), preferred_element_type=jnp.float32
    )
    tokens_grad_ref[0] = (back + gate).astype(tokens_grad_ref.dtype)
    left_term = lax.dot_general(
        grad_first, x_ref[0], (((1,), (1,)), ((), ())), preferred_element_type=jnp.float32
    )
    left_ref[0] = left_term * grad_unscale


def shards(tokens, cotangent, left_factor, right_factor):
    a_rows, block_len, _ = left_factor.shape
    b_rows = right_factor.shape[0]
    channels = tokens.shape[2]
    devices = block_len // b_rows
    if b_rows % 8 or a_rows % 8 or tokens.shape[0] != 1:
        return plain_shards(tokens, cotangent, left_factor, right_factor)
    head = a_rows // 8
    tail = a_rows - head
    x = tokens.reshape(a_rows, block_len, channels)
    g = cotangent.reshape(a_rows, block_len, channels)
    row_bytes = block_len * channels * 2
    row_flops = 2 * block_len * block_len * channels
    row = functools.partial(row_spec, block_len, channels)
    square = functools.partial(row_spec, block_len, block_len)
    split = functools.partial(split_spec, devices, b_rows, channels)

    def split_shape(n):
        return jax.ShapeDtypeStruct((devices, n, b_rows, channels), jnp.bfloat16)

    def first_part(lo, n, vmem_mib):
        return call(
            first_kernel,
            n,
            [square(lo), row(lo)],
            split(),
            split_shape(n),
            (n * row_flops, 2 * n * row_bytes),
            vmem_mib=vmem_mib,
        )(left_factor, x)

    first_0 = exchange(first_part(0, head, 60))
    first_1 = exchange(after(first_part(head, tail, 48), first_0))
    grad_second = call(
        grad_second_kernel,
        a_rows,
        [row(), row()],
        split(),
        split_shape(a_rows),
        (a_rows * row_bytes * 5, 3 * a_rows * row_bytes),
    )(x, g)
    grad_cols = exchange(after(grad_second, first_0)).reshape(devices * a_rows, b_rows, channels)
    first_cols = jnp.concatenate([first_0, first_1], axis=1).reshape(
        devices * a_rows, b_rows, channels
    )
    second_cols = jnp.einsum(
        "bij,jbd->ibd", right_factor, first_cols, preferred_element_type=jnp.float32
    ).astype(jnp.bfloat16)
    second = exchange(second_cols.reshape(devices, a_rows, b_rows, channels))
    grad_rows = (
        jnp.einsum("bij,ibd->jbd", right_factor, grad_cols, preferred_element_type=jnp.float32)
        .astype(jnp.bfloat16)
        .reshape(devices, a_rows, b_rows, channels)
    )
    grad_first_0 = exchange(grad_rows[:, :tail])
    right_term = jnp.einsum(
        "ibd,jbd->bij", grad_cols, first_cols, preferred_element_type=jnp.float32
    )
    right_grad = (
        lax.psum_scatter(right_term, "batch", scatter_dimension=1, tiled=True) * grad_unscale
    )
    output = call(
        output_kernel,
        a_rows,
        [row(), split()],
        row(),
        jax.ShapeDtypeStruct(x.shape, jnp.bfloat16),
        (a_rows * row_bytes * 5, 3 * a_rows * row_bytes),
    )(x, second)
    grad_first_0, output, right_grad = lax.optimization_barrier(
        (grad_first_0, output, right_grad)
    )
    grad_first_1 = exchange(after(grad_rows[:, tail:], grad_first_0))

    def last_part(lo, n, grad_first, *held):
        return call(
            last_kernel,
            n,
            [square(lo), row(lo), row(lo), split(lo), split()]
            + [pl.BlockSpec(memory_space=pl.ANY)] * len(held),
            (row(lo), square(lo)),
            (
                jax.ShapeDtypeStruct(x.shape, jnp.bfloat16),
                jax.ShapeDtypeStruct(left_factor.shape, jnp.float32),
            ),
            (2 * n * row_flops, 5 * n * row_bytes),
            {5 + k: k for k in range(len(held))},
        )(left_factor, x, g, second, grad_first, *held)

    held = last_part(0, tail, grad_first_0)
    grad_first_1, *held = lax.optimization_barrier((grad_first_1, *held))
    tokens_grad, left_term = last_part(tail, head, grad_first_1, *held)
    left_grad = lax.psum_scatter(left_term, "batch", scatter_dimension=1, tiled=True)
    return (output.reshape(tokens.shape), tokens_grad.reshape(tokens.shape), left_grad, right_grad)


def solution(mesh):
    return jax.shard_map(
        shards,
        mesh=mesh,
        in_specs=(
            P("batch", "seq", None),
            P("batch", "seq", None),
            P("seq", None, None),
            P("seq", None, None),
        ),
        out_specs=(
            P("batch", "seq", None),
            P("batch", "seq", None),
            P("seq", "batch", None),
            P("seq", "batch", None),
        ),
        check_vma=False,
    )
```

```python
import functools

import jax
import jax.numpy as jnp
from jax import lax
from jax.experimental import pallas as pl
from jax.experimental.pallas import tpu as pltpu
from jax.sharding import PartitionSpec as P

grad_unscale = 1.0 / 32.0


def plain_shards(tokens, cotangent, left_factor, right_factor):
    a_rows = left_factor.shape[0]
    block_len = left_factor.shape[1]
    channels = tokens.shape[2]
    blocks = tokens.reshape(a_rows, block_len, channels)
    upstream = cotangent.reshape(a_rows, block_len, channels).astype(jnp.float32)
    tokens_f = blocks.astype(jnp.float32)
    gate_sig = jax.nn.sigmoid(tokens_f)
    silu_x = tokens_f * gate_sig
    first = jnp.einsum(
        "apq,aqd->apd", left_factor, blocks, preferred_element_type=jnp.float32
    ).astype(jnp.bfloat16)
    grad_second = (upstream * silu_x).astype(jnp.bfloat16)
    first_cols = lax.all_to_all(first, "seq", split_axis=1, concat_axis=0, tiled=True)
    first_cols, second = (
        first_cols,
        lax.all_to_all(
            jnp.einsum(
                "bij,jbd->ibd", right_factor, first_cols, preferred_element_type=jnp.float32
            ).astype(jnp.bfloat16),
            "seq",
            split_axis=0,
            concat_axis=1,
            tiled=True,
        ),
    )
    grad_cols = lax.all_to_all(grad_second, "seq", split_axis=1, concat_axis=0, tiled=True)
    grad_cols, grad_first = (
        grad_cols,
        lax.all_to_all(
            jnp.einsum(
                "bij,ibd->jbd", right_factor, grad_cols, preferred_element_type=jnp.float32
            ).astype(jnp.bfloat16),
            "seq",
            split_axis=0,
            concat_axis=1,
            tiled=True,
        ),
    )
    right_term = jnp.einsum(
        "ibd,jbd->bij", grad_cols, first_cols, preferred_element_type=jnp.float32
    )
    right_grad = (
        lax.psum_scatter(right_term, "batch", scatter_dimension=1, tiled=True) * grad_unscale
    )
    second_f = second.astype(jnp.float32)
    output = (second_f * silu_x).astype(jnp.bfloat16)
    gate_grad = upstream * second_f * gate_sig * (1.0 + tokens_f * (1.0 - gate_sig))
    tokens_grad = (
        jnp.einsum("apq,apd->aqd", left_factor, grad_first, preferred_element_type=jnp.float32)
        + gate_grad
    ).astype(jnp.bfloat16)
    left_term = jnp.einsum("apd,aqd->apq", grad_first, blocks, preferred_element_type=jnp.float32)
    left_grad = lax.psum_scatter(left_term, "batch", scatter_dimension=1, tiled=True) * grad_unscale
    return (output.reshape(tokens.shape), tokens_grad.reshape(tokens.shape), left_grad, right_grad)


def exchange(parts):
    return lax.all_to_all(parts, "seq", split_axis=0, concat_axis=0, tiled=True)


def after(value, *others):
    return lax.optimization_barrier((value,) + others)[0]


def call(kernel, n, in_specs, out_specs, out_shape, cost, aliases=None, vmem_mib=48):
    return pl.pallas_call(
        kernel,
        grid=(n,),
        in_specs=in_specs,
        out_specs=out_specs,
        out_shape=out_shape,
        input_output_aliases=aliases or {},
        cost_estimate=pl.CostEstimate(flops=cost[0], bytes_accessed=cost[1], transcendentals=0),
        compiler_params=pltpu.CompilerParams(vmem_limit_bytes=vmem_mib * 1024 * 1024),
    )


def row_spec(rows, columns, lo=0):
    return pl.BlockSpec((1, rows, columns), lambda a: (a + lo, 0, 0))


def split_spec(devices, b_rows, channels, lo=0):
    return pl.BlockSpec((devices, 1, b_rows, channels), lambda a: (0, a + lo, 0, 0))


def store_split(out_ref, value):
    devices, _, b_rows, channels = out_ref.shape
    out_ref[:, 0] = value.reshape(devices, b_rows, channels).astype(out_ref.dtype)


def load_split(in_ref):
    devices, _, b_rows, channels = in_ref.shape
    return in_ref[:, 0].astype(jnp.float32).reshape(devices * b_rows, channels)


def first_kernel(l_ref, x_ref, o_ref):
    devices, rows, b_rows, channels = o_ref.shape
    for k in range(rows):
        first = jnp.dot(l_ref[k], x_ref[k], preferred_element_type=jnp.float32)
        o_ref[:, k] = first.reshape(devices, b_rows, channels).astype(o_ref.dtype)


def grad_second_kernel(x_ref, g_ref, o_ref):
    x = x_ref[0].astype(jnp.float32)
    store_split(o_ref, g_ref[0].astype(jnp.float32) * (x * jax.nn.sigmoid(x)))


def output_kernel(x_ref, second_ref, o_ref):
    x = x_ref[0].astype(jnp.float32)
    o_ref[0] = (load_split(second_ref) * (x * jax.nn.sigmoid(x))).astype(o_ref.dtype)


def last_kernel(l_ref, x_ref, g_ref, second_ref, grad_ref, *rest):
    tokens_grad_ref, left_ref = rest[-2:]
    x = x_ref[0].astype(jnp.float32)
    s = jax.nn.sigmoid(x)
    gate = g_ref[0].astype(jnp.float32) * load_split(second_ref) * s * (1.0 + x * (1.0 - s))
    grad_first = load_split(grad_ref).astype(jnp.bfloat16)
    back = lax.dot_general(
        l_ref[0], grad_first, (((0,), (0,)), ((), ())), preferred_element_type=jnp.float32
    )
    tokens_grad_ref[0] = (back + gate).astype(tokens_grad_ref.dtype)
    left_term = lax.dot_general(
        grad_first, x_ref[0], (((1,), (1,)), ((), ())), preferred_element_type=jnp.float32
    )
    left_ref[0] = left_term * grad_unscale


def shards(tokens, cotangent, left_factor, right_factor):
    a_rows, block_len, _ = left_factor.shape
    b_rows = right_factor.shape[0]
    channels = tokens.shape[2]
    devices = block_len // b_rows
    if b_rows % 8 or a_rows % 8 or tokens.shape[0] != 1:
        return plain_shards(tokens, cotangent, left_factor, right_factor)
    head = a_rows // 8
    tail = a_rows - head
    step = a_rows // 2
    x = tokens.reshape(a_rows, block_len, channels)
    g = cotangent.reshape(a_rows, block_len, channels)
    row_bytes = block_len * channels * 2
    row_flops = 2 * block_len * block_len * channels
    row = functools.partial(row_spec, block_len, channels)
    square = functools.partial(row_spec, block_len, block_len)
    split = functools.partial(split_spec, devices, b_rows, channels)

    def split_shape(n):
        return jax.ShapeDtypeStruct((devices, n, b_rows, channels), jnp.bfloat16)

    first = call(
        first_kernel,
        a_rows // step,
        [
            pl.BlockSpec((step, block_len, block_len), lambda a: (a, 0, 0)),
            pl.BlockSpec((step, block_len, channels), lambda a: (a, 0, 0)),
        ],
        pl.BlockSpec((devices, step, b_rows, channels), lambda a: (0, a, 0, 0)),
        split_shape(a_rows),
        (a_rows * row_flops, 2 * a_rows * row_bytes),
        vmem_mib=60,
    )(left_factor, x)
    first_cols = exchange(first).reshape(devices * a_rows, b_rows, channels)
    grad_second = call(
        grad_second_kernel,
        a_rows,
        [row(), row()],
        split(),
        split_shape(a_rows),
        (a_rows * row_bytes * 5, 3 * a_rows * row_bytes),
    )(x, g)
    grad_cols = exchange(grad_second).reshape(devices * a_rows, b_rows, channels)
    second_cols = jnp.einsum(
        "bij,jbd->ibd", right_factor, first_cols, preferred_element_type=jnp.float32
    ).astype(jnp.bfloat16)
    second = exchange(second_cols.reshape(devices, a_rows, b_rows, channels))
    grad_rows = (
        jnp.einsum("bij,ibd->jbd", right_factor, grad_cols, preferred_element_type=jnp.float32)
        .astype(jnp.bfloat16)
        .reshape(devices, a_rows, b_rows, channels)
    )
    grad_first_0 = exchange(grad_rows[:, :tail])
    right_term = jnp.einsum(
        "ibd,jbd->bij", grad_cols, first_cols, preferred_element_type=jnp.float32
    )
    right_grad = (
        lax.psum_scatter(right_term, "batch", scatter_dimension=1, tiled=True) * grad_unscale
    )
    output = call(
        output_kernel,
        a_rows,
        [row(), split()],
        row(),
        jax.ShapeDtypeStruct(x.shape, jnp.bfloat16),
        (a_rows * row_bytes * 5, 3 * a_rows * row_bytes),
    )(x, second)
    grad_first_0, output, right_grad = lax.optimization_barrier(
        (grad_first_0, output, right_grad)
    )
    grad_first_1 = exchange(after(grad_rows[:, tail:], grad_first_0))

    def last_part(lo, n, grad_first, *held):
        return call(
            last_kernel,
            n,
            [square(lo), row(lo), row(lo), split(lo), split()]
            + [pl.BlockSpec(memory_space=pl.ANY)] * len(held),
            (row(lo), square(lo)),
            (
                jax.ShapeDtypeStruct(x.shape, jnp.bfloat16),
                jax.ShapeDtypeStruct(left_factor.shape, jnp.float32),
            ),
            (2 * n * row_flops, 5 * n * row_bytes),
            {5 + k: k for k in range(len(held))},
        )(left_factor, x, g, second, grad_first, *held)

    held = last_part(0, tail, grad_first_0)
    grad_first_1, *held = lax.optimization_barrier((grad_first_1, *held))
    tokens_grad, left_term = last_part(tail, head, grad_first_1, *held)
    left_grad = lax.psum_scatter(left_term, "batch", scatter_dimension=1, tiled=True)
    return (output.reshape(tokens.shape), tokens_grad.reshape(tokens.shape), left_grad, right_grad)


def solution(mesh):
    return jax.shard_map(
        shards,
        mesh=mesh,
        in_specs=(
            P("batch", "seq", None),
            P("batch", "seq", None),
            P("seq", None, None),
            P("seq", None, None),
        ),
        out_specs=(
            P("batch", "seq", None),
            P("batch", "seq", None),
            P("seq", "batch", None),
            P("seq", "batch", None),
        ),
        check_vma=False,
    )
```
